32 devices in a mesh: group: 2 (over x), wide: 16 (over z, y, core).
Axes of the slice: x: 2, y: 2, z: 4, core: 2. Of those that a mesh axis runs over, the one named last changes fastest.
Arguments:
- tokens: bfloat16 [32, 18432], P('group', 'wide'), parts along dimension 0, may hold values from -6 to 6
- norm_gain: float32 [18432], P('wide'), may hold values from 0.1 to 1.9
- w_query: bfloat16 [18432, 12288], P('wide'), may hold values from -0.046875 to 0.046875
- w_keyval: bfloat16 [18432, 512], P('wide'), may hold values from -0.046875 to 0.046875
- w_out: bfloat16 [12288, 18432], P(None, 'wide'), may hold values from -0.0546875 to 0.0546875
- cache: bfloat16 [32, 4096, 512], P(('group', 'wide')), parts along dimension 0, may hold values from -1000 to 1000, as said below
- lengths: int32 [32], P(('group', 'wide')), parts along dimension 0, may hold values from 256 to 4096, as said below
Outputs:
- hidden: bfloat16 [32, 18432], P('group', 'wide'), parts along dimension 0
- fresh: bfloat16 [32, 1, 512], P(('group', 'wide')), parts along dimension 0
The draws below stay inside these ranges and needn't reach their ends.
There are 2 independent parts, one for each index of `group`. The reference program is written for one: setup_inputs(seed, part) draws one part's arguments, and reference() takes and returns one part's arrays. A program takes and returns all parts, laid end to end along the dimension named above; an argument that names none is the same for every part. Nothing has to cross between parts.
Inputs may be any that keep to these rules, and one draw needn't show every extreme that they name: `lengths`: every row's length lies between 256 and 4096; some row has length exactly 4096 and some row exactly 256. `cache`: finite entries.
All inputs are finite; a program needn't handle non-finite values.
Results may differ from the reference program's by a relative error of at most 0.0059.
Values may be sent and summed in bfloat16 or wider, within the bound.
A program may use at most 128 MiB of HBM per device.

```python
import jax
import jax.numpy as jnp
from jax import lax

D = 18432
HEADS = 48
HEAD = 256
CACHE = 4096
SHORT = 256
STEPS = 1
ROWS = 16


def draw_cache(key, part):
    key = jax.random.fold_in(key, 11)
    base = jnp.clip(jax.random.normal(key, (ROWS, CACHE, 2 * HEAD), jnp.float32), -6.0, 6.0)
    return base.astype(jnp.bfloat16)


def draw_lengths(key, part):
    key = jax.random.fold_in(key, 5)
    first, second, third, fourth = jax.random.split(key, 4)
    left = jax.random.randint(first, (ROWS,), 0, CACHE)
    right = jax.random.randint(second, (ROWS,), 0, CACHE)
    raw = jnp.minimum(SHORT + left * right // CACHE, CACHE)
    longest = jax.random.randint(third, (), 0, ROWS)
    shortest = (longest + 1 + jax.random.randint(fourth, (), 0, ROWS - 1)) % ROWS
    places = jnp.arange(ROWS)
    raw = jnp.where(places == longest, CACHE, raw)
    raw = jnp.where(places == shortest, SHORT, raw)
    return raw.astype(jnp.int32)


def with_spikes(entries, own_key, source, target, parts, factor):
    owner, partner = [(jnp.arange(entries.shape[axis_at]) // (entries.shape[axis_at] // parts)).reshape([-1 if axis == axis_at else 1 for axis in range(entries.ndim)]) for axis_at in (source, target)]
    chosen = jax.random.permutation(own_key, parts)[partner]
    strong = (owner == chosen) | (owner == (partner + parts // 2) % parts)
    return jnp.where(strong, factor * entries, entries)


def block_scale(own_key, extent, cuts, low, largest):
    def one(dim, blocks):
        heights = jax.random.uniform(jax.random.fold_in(jax.random.fold_in(own_key, 6), dim), (blocks,), jnp.float32, low / len(cuts), largest / len(cuts))
        return jnp.repeat(jnp.exp(heights), extent[dim] // blocks).reshape((-1,) + (1,) * (len(extent) - dim - 1))

    level = one(*cuts[0])
    for cut in cuts[1:]:
        level = level * one(*cut)
    return level


def centred(key, extent, deviation, bound, cuts=(), held_as=jnp.bfloat16):
    entries = jax.random.normal(key, extent, jnp.float32) * deviation
    if len(cuts) > 0:
        entries = block_scale(key, extent, cuts, -0.22, 0.18) * entries
    return jnp.clip(entries, min=-bound, max=bound).astype(held_as)


def heavy_noise(key, dims, deviation, most, pieces, heavy, kind=jnp.bfloat16):
    result = deviation * jax.random.normal(key, dims, jnp.float32)
    if pieces:
        result = result * block_scale(key, dims, pieces, -0.22, 0.18)
    return jnp.clip(with_spikes(result, jax.random.fold_in(key, 3), *heavy), -most, most).astype(kind)


def setup_inputs(seed: int = 0, part: int = 0) -> dict:
    splits = jax.random.split(jax.random.key(seed), 8)
    part_keys = jax.random.split(jax.random.fold_in(splits[7], part), 8)
    return {
        "tokens": heavy_noise(part_keys[0], (ROWS, D), 1.0, 6.0, ((1, 16),), (1, 0, 16, 2.0)),
        "norm_gain": jnp.clip(1.0 + 0.18 * jax.random.normal(splits[1], (D,), jnp.float32), 0.1, 1.9),
        "w_query": centred(splits[2], (D, HEADS * HEAD), D ** -0.5, 0.046875, ((0, 16),)),
        "w_keyval": centred(splits[3], (D, 2 * HEAD), D ** -0.5, 0.046875, ((0, 16),)),
        "w_out": centred(splits[4], (HEADS * HEAD, D), (HEADS * HEAD) ** -0.5, 0.0546875, ((1, 16),)),
        "cache": draw_cache(jax.random.fold_in(jax.random.fold_in(splits[7], part), 71), part),
        "lengths": draw_lengths(jax.random.fold_in(jax.random.fold_in(splits[7], part), 71), part),
    }


def attend_row(query_row, cache_row, fresh_row, length, step):
    heads_q = query_row.reshape(HEADS, HEAD).astype(jnp.float32)
    keys = cache_row[:, :HEAD].astype(jnp.float32)
    values = cache_row[:, HEAD:].astype(jnp.float32)
    new_keys = fresh_row[:, :HEAD].astype(jnp.float32)
    new_values = fresh_row[:, HEAD:].astype(jnp.float32)
    factor = HEAD ** (-0.5)
    old_mask = (jnp.arange(CACHE) < length)[None, :]
    new_mask = (jnp.arange(STEPS) <= step)[None, :]
    old_scores = jnp.where(old_mask, jnp.dot(heads_q, keys.T) * factor, -1e+30)
    new_scores = jnp.where(new_mask, jnp.dot(heads_q, new_keys.T) * factor, -1e+30)
    top = jnp.maximum(lax.optimization_barrier(jnp.max(old_scores, axis=1)), lax.optimization_barrier(jnp.max(new_scores, axis=1)))
    old_exp = jnp.where(old_mask, jnp.exp(old_scores - top[:, None]), 0.0)
    new_exp = jnp.where(new_mask, jnp.exp(new_scores - top[:, None]), 0.0)
    total = lax.optimization_barrier(jnp.sum(old_exp, axis=1)) + lax.optimization_barrier(jnp.sum(new_exp, axis=1))
    old_w = lax.optimization_barrier(old_exp.astype(jnp.bfloat16)).astype(jnp.float32)
    new_w = lax.optimization_barrier(new_exp.astype(jnp.bfloat16)).astype(jnp.float32)
    summed = jnp.dot(old_w, values) + jnp.dot(new_w, new_values)
    return (summed / total[:, None]).reshape(HEADS * HEAD).astype(jnp.bfloat16)

def reference(tokens, norm_gain, w_query, w_keyval, w_out, cache, lengths):
    state = tokens.astype(jnp.float32)
    fresh = jnp.zeros((ROWS, STEPS, 2 * HEAD), jnp.bfloat16)
    for step in range(STEPS):
        sumsq = lax.optimization_barrier(jnp.sum(state * state, axis=1))
        scale = lax.rsqrt(sumsq / D + 1e-06)
        scaled_in = (state * norm_gain[None, :]).astype(jnp.bfloat16)
        query = (jnp.dot(scaled_in, w_query, preferred_element_type=jnp.float32) * scale[:, None]).astype(jnp.bfloat16)
        keyval = (jnp.dot(scaled_in, w_keyval, preferred_element_type=jnp.float32) * scale[:, None]).astype(jnp.bfloat16)
        fresh = fresh.at[:, step].set(keyval)
        attended = lax.map(lambda item: attend_row(item[0], item[1], item[2], item[3], step), (query, cache, fresh, lengths))
        state = state + jnp.dot(attended, w_out, preferred_element_type=jnp.float32)
    return (state.astype(jnp.bfloat16), fresh)
```

```python
import functools

import jax
import jax.numpy as jnp
from jax import lax
from jax.experimental import pallas as pl
from jax.experimental.pallas import tpu as pltpu
from jax.sharding import PartitionSpec as P

MESH = pl.DeviceIdType.MESH
F32 = jnp.float32
BF16 = jnp.bfloat16
HEAD = 256
HALF = 128
GROUP = 8
SLOTS = 3
OUT_PIECES = 6


def layer_kernel(
    eps, factor, chips,
    len_ref, tokens_ref, gain_ref, wq_ref, wkv_ref, wo_ref, cache_ref,
    hidden_ref, fresh_ref,
    scaled, wq_buf, wkv_buf, wo_buf, cache_buf,
    part, pair_send, pair_recv, sums, far_send, far_recv,
    kv_part, kv_pair_send, kv_pair_recv, kv_sums, kv_far_send, kv_far_recv,
    query, gathered, wide32,
    wq_sem, wkv_sem, wo_sem, cache_sem,
    pair_ssem, pair_rsem, far_ssem, far_rsem,
    row_ssem, row_rsem, twin_ssem, twin_rsem,
):
    rows, width = tokens_ref.shape
    chunks = wq_ref.shape[1] // (GROUP * HEAD)
    heads = wq_ref.shape[1] // HEAD
    piece = wo_ref.shape[0] // OUT_PIECES
    me = lax.axis_index("wide")
    chip, core = me // 2, me % 2
    twin = chip * 2 + 1 - core

    def peer(d):
        return lax.rem(chip + d, chips)

    def row_piece(r):
        return pl.ds(pl.multiple_of(r * 2 * GROUP, 2 * GROUP), 2 * GROUP)

    def wq_copy(j):
        return pltpu.make_async_copy(
            wq_ref.at[:, pl.ds(j * GROUP * HEAD, GROUP * HEAD)], wq_buf.at[j % SLOTS], wq_sem.at[j % SLOTS]
        )

    def wo_copy(i):
        at = pl.ds(i * piece, piece)
        return pltpu.make_async_copy(wo_ref.at[at], wo_buf.at[at], wo_sem.at[i])

    wkv_copy = pltpu.make_async_copy(wkv_ref, wkv_buf, wkv_sem)
    cache_copy = pltpu.make_async_copy(cache_ref.at[0], cache_buf, cache_sem)

    wkv_copy.start()
    for j in range(SLOTS):
        wq_copy(j).start()

    barrier = pltpu.get_barrier_semaphore()
    pl.semaphore_signal(barrier, inc=1, device_id={"wide": twin}, device_id_type=MESH)
    for d in range(1, chips):
        pl.semaphore_signal(barrier, inc=1, device_id={"wide": peer(d) * 2 + core}, device_id_type=MESH)

    state = tokens_ref[...].astype(F32)
    sumsq = jnp.sum(state * state, axis=1, keepdims=True)
    scaled[...] = (state * gain_ref[...]).astype(BF16)
    pl.semaphore_wait(barrier, chips)

    def pair_copy(s):
        if s == 0:
            src, dst = kv_pair_send, kv_pair_recv
        else:
            src, dst = pair_send.at[s - 1], pair_recv.at[s - 1]
        return pltpu.make_async_remote_copy(
            src_ref=src, dst_ref=dst, send_sem=pair_ssem.at[s], recv_sem=pair_rsem.at[s],
            device_id={"wide": twin}, device_id_type=MESH,
        )

    def far_copy(s, d):
        if s == 0:
            src, dst = kv_far_send.at[d - 1], kv_far_recv.at[d - 1]
        else:
            src, dst = far_send.at[s - 1, d - 1], far_recv.at[s - 1, d - 1]
        return pltpu.make_async_remote_copy(
            src_ref=src, dst_ref=dst, send_sem=far_ssem.at[s, d - 1], recv_sem=far_rsem.at[s, d - 1],
            device_id={"wide": peer(d) * 2 + core}, device_id_type=MESH,
        )

    def combine(s):
        pair_copy(s).wait_recv()
        if s == 0:
            kv_sums[...] = kv_part[:, core] + kv_pair_recv[...]
            for d in range(1, chips):
                kv_far_send[d - 1] = kv_sums[peer(d)]
        else:
            for k in range(chips):
                sums[s - 1, k] = part[s - 1, row_piece(2 * k + core), :] + pair_recv[s - 1, k].astype(F32)
            for d in range(1, chips):
                far_send[s - 1, d - 1] = sums[s - 1, peer(d)].astype(BF16)
        for d in range(1, chips):
            far_copy(s, d).start()

    wkv_copy.wait()
    keyval = jnp.dot(scaled[...], wkv_buf[...], preferred_element_type=F32)
    for r in range(rows):
        at = (r // 2, r % 2)
        for n in range(4):
            kv_part[at[0], at[1], n : n + 1, :] = keyval[r : r + 1, n * HALF : (n + 1) * HALF]
        kv_part[at[0], at[1], 4:5, :] = jnp.broadcast_to(sumsq[r : r + 1], (1, HALF))
        kv_part[at[0], at[1], 5:8, :] = jnp.zeros((3, HALF), F32)
    kv_pair_send[...] = kv_part[:, 1 - core]
    pair_copy(0).start()

    for j in range(chunks):
        slot = j % SLOTS
        wq_copy(j).wait()

        def project(h, carry, slot=slot, j=j):
            at = pl.ds(pl.multiple_of(h * HEAD, HEAD), HEAD)
            got = jnp.dot(scaled[...], wq_buf[slot, :, at], preferred_element_type=F32)
            part[j, pl.ds(h, rows, stride=2 * GROUP), :] = got[:, :HALF]
            part[j, pl.ds(h + GROUP, rows, stride=2 * GROUP), :] = got[:, HALF:]
            return carry

        lax.fori_loop(0, GROUP, project, 0)
        if j + SLOTS < chunks:
            wq_copy(j + SLOTS).start()
        elif j + SLOTS == chunks:
            cache_copy.start()
            for i in range(OUT_PIECES):
                wo_copy(i).start()
        for k in range(chips):
            pair_send[j, k] = part[j, row_piece(2 * k + 1 - core), :].astype(BF16)
        pair_copy(j + 1).start()
        combine(j)
    combine(chunks)

    for d in range(1, chips):
        far_copy(0, d).wait_recv()
    total = kv_sums[chip]
    for d in range(1, chips):
        total = total + kv_far_recv[d - 1]
    scale = lax.rsqrt(total[4:5, :1] / (width * 2 * chips) + eps)
    keyval = (total[0:4] * scale).astype(BF16).astype(F32)
    fresh_ref[...] = keyval
    for j in range(chunks):
        for d in range(1, chips):
            far_copy(j + 1, d).wait_recv()
        mine = sums[j, chip]
        for d in range(1, chips):
            mine = mine + far_recv[j, d - 1].astype(F32)
        query[j * GROUP : (j + 1) * GROUP, :HALF] = mine[:GROUP]
        query[j * GROUP : (j + 1) * GROUP, HALF:] = mine[GROUP:]

    heads_q = (query[...] * scale).astype(BF16)
    new_key = jnp.concatenate([keyval[0:1], keyval[1:2]], axis=1)
    new_value = jnp.concatenate([keyval[2:3], keyval[3:4]], axis=1)
    new_score = jnp.sum(heads_q.astype(F32) * new_key, axis=1, keepdims=True) * factor
    cache_copy.wait()
    scores = lax.dot_general(
        heads_q, cache_buf[:, :HEAD], (((1,), (1,)), ((), ())), preferred_element_type=F32
    ) * factor
    valid = lax.broadcasted_iota(jnp.int32, scores.shape, 1) < len_ref[0]
    scores = jnp.where(valid, scores, -1e30)
    top = jnp.maximum(jnp.max(scores, axis=1, keepdims=True), new_score)
    exps = jnp.where(valid, jnp.exp(scores - top), 0.0)
    new_exp = jnp.exp(new_score - top)
    norm = jnp.sum(exps, axis=1, keepdims=True) + new_exp
    summed = jnp.dot(exps.astype(BF16), cache_buf[:, HEAD:], preferred_element_type=F32)
    summed = summed + new_exp.astype(BF16).astype(F32) * new_value
    gathered[me] = (summed / norm).astype(BF16)

    def row_copy(d):
        return pltpu.make_async_remote_copy(
            src_ref=gathered.at[me], dst_ref=gathered.at[me],
            send_sem=row_ssem.at[d - 1], recv_sem=row_rsem.at[d - 1],
            device_id={"wide": peer(d) * 2 + core}, device_id_type=MESH,
        )

    def twin_copy(d):
        at = peer(d) * 2 + core
        return pltpu.make_async_remote_copy(
            src_ref=gathered.at[at], dst_ref=gathered.at[at],
            send_sem=twin_ssem.at[d], recv_sem=twin_rsem.at[d],
            device_id={"wide": twin}, device_id_type=MESH,
        )

    for d in range(1, chips):
        row_copy(d).start()
    twin_copy(0).start()
    for d in range(chips - 1, 0, -1):
        row_copy(d).wait_recv()
        twin_copy(chips - d).start()
    for d in range(chips):
        twin_copy(d).wait_recv()

    wide32[0] = gathered[:, :, :HALF].astype(F32).reshape(rows * heads, HALF)
    wide32[1] = gathered[:, :, HALF:].astype(F32).reshape(rows * heads, HALF)

    def output(h, acc):
        at = pl.ds(h, rows, stride=heads)
        low = wide32[0, at, :].astype(BF16)
        high = wide32[1, at, :].astype(BF16)
        lhs = jnp.concatenate([low, high], axis=1)
        rhs = wo_buf[pl.ds(pl.multiple_of(h * HEAD, HEAD), HEAD), :]
        return acc + jnp.dot(lhs, rhs, preferred_element_type=F32)

    acc = tokens_ref[...].astype(F32)
    per = heads // OUT_PIECES
    for i in range(OUT_PIECES):
        wo_copy(i).wait()
        acc = lax.fori_loop(i * per, (i + 1) * per, output, acc)
    hidden_ref[...] = acc.astype(BF16)

    for s in range(chunks + 1):
        pair_copy(s).wait_send()
        for d in range(1, chips):
            far_copy(s, d).wait_send()
    for d in range(1, chips):
        row_copy(d).wait_send()
    for d in range(chips):
        twin_copy(d).wait_send()


def fused(lengths, tokens, norm_gain, w_query, w_keyval, w_out, cache):
    count = lax.axis_size("wide")
    chips = count // 2
    rows, width = tokens.shape
    heads = w_query.shape[1] // HEAD
    chunks = heads // GROUP
    positions = cache.shape[1]
    vmem = pl.BlockSpec(memory_space=pltpu.VMEM)
    hbm = pl.BlockSpec(memory_space=pl.ANY)
    dma = pltpu.SemaphoreType.DMA
    kernel = functools.partial(layer_kernel, 1e-06, HEAD ** (-0.5), chips)
    hidden, keyval = pl.pallas_call(
        kernel,
        out_shape=(
            jax.ShapeDtypeStruct((rows, width), BF16),
            jax.ShapeDtypeStruct((4, HALF), F32),
        ),
        in_specs=[pl.BlockSpec(memory_space=pltpu.SMEM), vmem, vmem, hbm, hbm, hbm, hbm],
        out_specs=(vmem, vmem),
        scratch_shapes=[
            pltpu.VMEM((rows, width), BF16),
            pltpu.VMEM((SLOTS, width, GROUP * HEAD), BF16),
            pltpu.VMEM(w_keyval.shape, BF16),
            pltpu.VMEM(w_out.shape, BF16),
            pltpu.VMEM(cache.shape[1:], BF16),
            pltpu.VMEM((chunks, rows * 2 * GROUP, HALF), F32),
            pltpu.VMEM((chunks, chips, 2 * GROUP, HALF), BF16),
            pltpu.VMEM((chunks, chips, 2 * GROUP, HALF), BF16),
            pltpu.VMEM((chunks, chips, 2 * GROUP, HALF), F32),
            pltpu.VMEM((chunks, chips - 1, 2 * GROUP, HALF), BF16),
            pltpu.VMEM((chunks, chips - 1, 2 * GROUP, HALF), BF16),
            pltpu.VMEM((chips, 2, 8, HALF), F32),
            pltpu.VMEM((chips, 8, HALF), F32),
            pltpu.VMEM((chips, 8, HALF), F32),
            pltpu.VMEM((chips, 8, HALF), F32),
            pltpu.VMEM((chips - 1, 8, HALF), F32),
            pltpu.VMEM((chips - 1, 8, HALF), F32),
            pltpu.VMEM((heads, HEAD), F32),
            pltpu.VMEM((rows, heads, HEAD), BF16),
            pltpu.VMEM((2, rows * heads, HALF), F32),
            dma((SLOTS,)), dma, dma((OUT_PIECES,)), dma,
            dma((chunks + 1,)), dma((chunks + 1,)),
            dma((chunks + 1, chips - 1)), dma((chunks + 1, chips - 1)),
            dma((chips - 1,)), dma((chips - 1,)), dma((chips,)), dma((chips,)),
        ],
        compiler_params=pltpu.CompilerParams(
            collective_id=0, has_side_effects=True, vmem_limit_bytes=60 * 1024 * 1024
        ),
        cost_estimate=pl.CostEstimate(
            flops=2 * rows * width * (w_query.shape[1] * 2) + 4 * w_query.shape[1] * positions,
            bytes_accessed=2 * (w_query.size + w_out.size + cache.size),
            transcendentals=heads * positions,
        ),
    )(lengths, tokens, norm_gain[None, :], w_query, w_keyval, w_out, cache)
    return hidden, keyval.reshape(1, 1, 4 * HALF).astype(BF16)


def masked_scores(heads_q, keys, valid, factor):
    scores = jnp.einsum("rhd,rld->rhl", heads_q, keys, preferred_element_type=F32) * factor
    return jnp.where(valid, scores, -1e30)


def attend(query, cache, fresh, lengths):
    own = query.shape[0]
    head = fresh.shape[2] // 2
    heads = query.shape[1] // head
    factor = head ** (-0.5)
    heads_q = query.reshape(own, heads, head)
    new_scores = masked_scores(heads_q, fresh[:, :, :head], True, factor)
    old_valid = (jnp.arange(cache.shape[1])[None, :] < lengths[:, None])[:, None, :]
    old_scores = masked_scores(heads_q, cache[:, :, :head], old_valid, factor)
    top = jnp.maximum(jnp.max(old_scores, axis=2), jnp.max(new_scores, axis=2))
    old_exp = jnp.where(old_valid, jnp.exp(old_scores - top[..., None]), 0.0)
    new_exp = jnp.exp(new_scores - top[..., None])
    total = jnp.sum(old_exp, axis=2) + jnp.sum(new_exp, axis=2)
    summed = jnp.einsum("rhl,rld->rhd", old_exp.astype(BF16), cache[:, :, head:], preferred_element_type=F32)
    summed = summed + jnp.einsum(
        "rhs,rsd->rhd", new_exp.astype(BF16), fresh[:, :, head:], preferred_element_type=F32
    )
    return (summed / total[..., None]).reshape(own, heads * head).astype(BF16)


def plain(lengths, tokens, norm_gain, w_query, w_keyval, w_out, cache):
    count = lax.axis_size("wide")
    own = tokens.shape[0] // count
    base_row = lax.axis_index("wide") * own
    state = tokens.astype(F32)
    scaled_in = (state * norm_gain[None, :]).astype(BF16)
    sumsq = lax.psum(jnp.sum(state * state, axis=1), "wide")
    sumsq = lax.dynamic_slice_in_dim(sumsq, base_row, own, 0)
    scale = lax.rsqrt(sumsq / (tokens.shape[1] * count) + 1e-06)[:, None]

    def project(weights):
        partial = jnp.dot(scaled_in, weights, preferred_element_type=F32)
        return (lax.psum_scatter(partial, "wide", scatter_dimension=0, tiled=True) * scale).astype(BF16)

    query = project(w_query)
    fresh = project(w_keyval)[:, None, :]
    attended = attend(query, cache, fresh, lengths)
    everything = lax.all_gather(attended, "wide", axis=0, tiled=True)
    state = state + jnp.dot(everything, w_out, preferred_element_type=F32)
    return state.astype(BF16), fresh


def on_device(tokens, norm_gain, w_query, w_keyval, w_out, cache, lengths):
    count = lax.axis_size("wide")
    fits = (
        tokens.shape[0] == count
        and count <= 16
        and tokens.shape[1] % HALF == 0
        and w_out.size + cache.size <= 18 * 1024 * 1024
    )
    body = fused if fits else plain
    return body(lengths, tokens, norm_gain, w_query, w_keyval, w_out, cache)


def solution(mesh):
    in_specs = (
        P("group", "wide"),
        P("wide"),
        P("wide", None),
        P("wide", None),
        P(None, "wide"),
        P(("group", "wide"), None, None),
        P(("group", "wide")),
    )
    out_specs = (P("group", "wide"), P(("group", "wide"), None, None))
    return jax.shard_map(
        on_device, mesh=mesh, in_specs=in_specs, out_specs=out_specs, check_vma=False
    )
```

```python
import functools

import jax
import jax.numpy as jnp
from jax import lax
from jax.experimental import pallas as pl
from jax.experimental.pallas import tpu as pltpu
from jax.sharding import PartitionSpec as P

MESH = pl.DeviceIdType.MESH
F32 = jnp.float32
BF16 = jnp.bfloat16
HEAD = 256
HALF = 128
GROUP = 8
PAIR = 2
TEAM = PAIR * GROUP
SLOTS = 3
OUT_PIECES = 6
COLUMNS = 4 * HEAD


def layer_kernel(
    eps, factor, chips,
    len_ref, tokens_ref, gain_ref, wq_ref, wkv_ref, wo_ref, cache_ref,
    hidden_ref, fresh_ref,
    scaled, wq_buf, wkv_buf, wo_buf, cache_buf,
    part, pair_send, pair_recv, sums, far_send, far_recv,
    kv_part, kv_pair_send, kv_pair_recv, kv_sums, kv_far_send, kv_far_recv,
    gathered, wide32,
    wq_sem, wkv_sem, wo_sem, cache_sem,
    pair_ssem, pair_rsem, far_ssem, far_rsem,
    row_ssem, row_rsem, twin_ssem, twin_rsem,
):
    rows, width = tokens_ref.shape
    chunks = wq_ref.shape[1] // (GROUP * HEAD)
    piece = wo_ref.shape[0] // OUT_PIECES
    me = lax.axis_index("wide")
    chip, core = me // 2, me % 2
    twin = chip * 2 + 1 - core

    def peer(d):
        found, bit = 0, 1
        while bit < chips:
            own = (chip // bit) % 2
            found = found + bit * (1 - own if d & bit else own)
            bit *= 2
        return found

    def row_piece(r):
        return pl.ds(pl.multiple_of(r * 2 * GROUP, 2 * GROUP), 2 * GROUP)

    def wq_copy(j):
        return pltpu.make_async_copy(
            wq_ref.at[:, pl.ds(j * GROUP * HEAD, GROUP * HEAD)], wq_buf.at[j % SLOTS], wq_sem.at[j % SLOTS]
        )

    def wo_copy(i):
        at = pl.ds(i * piece, piece)
        return pltpu.make_async_copy(wo_ref.at[at], wo_buf.at[at], wo_sem.at[i])

    wkv_copy = pltpu.make_async_copy(wkv_ref, wkv_buf, wkv_sem)
    cache_copy = pltpu.make_async_copy(cache_ref.at[0], cache_buf, cache_sem)

    wkv_copy.start()
    for j in range(SLOTS):
        wq_copy(j).start()

    barrier = pltpu.get_barrier_semaphore()
    pl.semaphore_signal(barrier, inc=1, device_id={"wide": twin}, device_id_type=MESH)
    for d in range(1, chips):
        pl.semaphore_signal(barrier, inc=1, device_id={"wide": peer(d) * 2 + core}, device_id_type=MESH)

    state = tokens_ref[...].astype(F32)
    sumsq = jnp.sum(state * state, axis=1, keepdims=True)
    for n in range(width // HALF):
        at = slice(n * HALF, (n + 1) * HALF)
        scaled[:, at] = (state[:, at] * gain_ref[n : n + 1, :]).astype(BF16)
    pl.semaphore_wait(barrier, chips)

    def pair_copy(s):
        if s == 0:
            src, dst = kv_pair_send, kv_pair_recv
        else:
            src, dst = pair_send.at[s - 1], pair_recv.at[s - 1]
        return pltpu.make_async_remote_copy(
            src_ref=src, dst_ref=dst, send_sem=pair_ssem.at[s], recv_sem=pair_rsem.at[s],
            device_id={"wide": twin}, device_id_type=MESH,
        )

    def far_copy(s, d):
        if s == 0:
            src, dst = kv_far_send.at[d - 1], kv_far_recv.at[d - 1]
        else:
            src, dst = far_send.at[s - 1, d - 1], far_recv.at[s - 1, d - 1]
        return pltpu.make_async_remote_copy(
            src_ref=src, dst_ref=dst, send_sem=far_ssem.at[s, d - 1], recv_sem=far_rsem.at[s, d - 1],
            device_id={"wide": peer(d) * 2 + core}, device_id_type=MESH,
        )

    def combine(s):
        pair_copy(s).wait_recv()
        if s == 0:
            kv_sums[...] = kv_part[:, core] + kv_pair_recv[...]
            for d in range(1, chips):
                kv_far_send[d - 1] = kv_sums[peer(d)]
        else:
            for k in range(chips):
                sums[s - 1, k] = part[s - 1, row_piece(2 * k + core), :] + pair_recv[s - 1, k].astype(F32)
            for d in range(1, chips):
                far_send[s - 1, d - 1] = sums[s - 1, peer(d)].astype(BF16)
        for d in range(chips - 1, 0, -1):
            far_copy(s, d).start()

    wkv_copy.wait()
    keyval = jnp.dot(scaled[...], wkv_buf[...], preferred_element_type=F32)
    for r in range(rows):
        at = (r // 2, r % 2)
        for n in range(4):
            kv_part[at[0], at[1], n : n + 1, :] = keyval[r : r + 1, n * HALF : (n + 1) * HALF]
        kv_part[at[0], at[1], 4:5, :] = jnp.broadcast_to(sumsq[r : r + 1], (1, HALF))
        kv_part[at[0], at[1], 5:8, :] = jnp.zeros((3, HALF), F32)
    kv_pair_send[...] = kv_part[:, 1 - core]
    pair_copy(0).start()

    def project(j):
        slot = j % SLOTS

        def columns(n, carry):
            at = pl.ds(pl.multiple_of(n * COLUMNS, COLUMNS), COLUMNS)
            got = jnp.dot(scaled[...], wq_buf[slot, :, at], preferred_element_type=F32)
            for i in range(COLUMNS // HEAD):
                h = n * (COLUMNS // HEAD) + i
                low = got[:, i * HEAD : i * HEAD + HALF]
                high = got[:, i * HEAD + HALF : (i + 1) * HEAD]
                part[j, pl.ds(h, rows, stride=2 * GROUP), :] = low
                part[j, pl.ds(h + GROUP, rows, stride=2 * GROUP), :] = high
            return carry

        lax.fori_loop(0, GROUP * HEAD // COLUMNS, columns, 0)

    def own_sums():
        for d in range(1, chips):
            far_copy(0, d).wait_recv()
        total = kv_sums[chip]
        for d in range(1, chips):
            total = total + kv_far_recv[d - 1]
        scale = lax.rsqrt(total[4:5, :1] / (width * 2 * chips) + eps)
        keyval = (total[0:4] * scale).astype(BF16)
        for n in range(4):
            fresh_ref[0, :, n * HALF : (n + 1) * HALF] = keyval[n : n + 1]
        keyval = keyval.astype(F32)
        new_key = jnp.concatenate([keyval[0:1], keyval[1:2]], axis=1)
        new_value = jnp.concatenate([keyval[2:3], keyval[3:4]], axis=1)
        return scale, new_key, new_value

    def own_query(j):
        for d in range(1, chips):
            far_copy(j + 1, d).wait_recv()
        mine = sums[j, chip]
        for d in range(1, chips):
            mine = mine + far_recv[j, d - 1].astype(F32)
        return jnp.concatenate([mine[:GROUP], mine[GROUP:]], axis=1)

    def attention(g):
        scale, new_key, new_value = new_token
        heads_q = jnp.concatenate([own_query(g * PAIR + i) for i in range(PAIR)], axis=0)
        heads_q = (heads_q * scale).astype(BF16)
        new_score = jnp.sum(heads_q.astype(F32) * new_key, axis=1, keepdims=True) * factor
        scores = lax.dot_general(
            heads_q, cache_buf[:, :HEAD], (((1,), (1,)), ((), ())), preferred_element_type=F32
        ) * factor
        valid = lax.broadcasted_iota(jnp.int32, scores.shape, 1) < len_ref[0]
        scores = jnp.where(valid, scores, -1e30)
        top = jnp.maximum(jnp.max(scores, axis=1, keepdims=True), new_score)
        exps = jnp.where(valid, jnp.exp(scores - top), 0.0)
        new_exp = jnp.exp(new_score - top)
        norm = jnp.sum(exps, axis=1, keepdims=True) + new_exp
        summed = jnp.dot(exps.astype(BF16), cache_buf[:, HEAD:], preferred_element_type=F32)
        summed = summed + new_exp.astype(BF16).astype(F32) * new_value
        gathered[g, me] = (summed / norm).astype(BF16)
        for d in range(chips - 1, 0, -1):
            row_copy(g, d).start()
        twin_copy(g, 0).start()

    def row_copy(g, d):
        return pltpu.make_async_remote_copy(
            src_ref=gathered.at[g, me], dst_ref=gathered.at[g, me],
            send_sem=row_ssem.at[g, d - 1], recv_sem=row_rsem.at[g, d - 1],
            device_id={"wide": peer(d) * 2 + core}, device_id_type=MESH,
        )

    def twin_copy(g, d):
        at = peer(d) * 2 + core
        return pltpu.make_async_remote_copy(
            src_ref=gathered.at[g, at], dst_ref=gathered.at[g, at],
            send_sem=twin_ssem.at[g, d], recv_sem=twin_rsem.at[g, d],
            device_id={"wide": twin}, device_id_type=MESH,
        )

    def share(g):
        for d in range(1, chips):
            row_copy(g, d).wait_recv()
            twin_copy(g, d).start()

    def output(g, acc):
        for d in range(chips):
            twin_copy(g, d).wait_recv()
        wide32[0] = gathered[g, :, :, :HALF].astype(F32).reshape(rows * TEAM, HALF)
        wide32[1] = gathered[g, :, :, HALF:].astype(F32).reshape(rows * TEAM, HALF)
        per = OUT_PIECES // teams
        count = COLUMNS // HEAD

        def step(n, acc):
            sides = []
            for i in range(count):
                at = pl.ds(n * count + i, rows, stride=TEAM)
                sides.append(wide32[0, at, :].astype(BF16))
                sides.append(wide32[1, at, :].astype(BF16))
            lhs = jnp.concatenate(sides, axis=1)
            at = pl.ds(pl.multiple_of(g * TEAM * HEAD + n * COLUMNS, COLUMNS), COLUMNS)
            return acc + jnp.dot(lhs, wo_buf[at, :], preferred_element_type=F32)

        steps = TEAM * HEAD // COLUMNS
        for i in range(per):
            wo_copy(g * per + i).wait()
            acc = lax.fori_loop(i * steps // per, (i + 1) * steps // per, step, acc)
        return acc

    teams = chunks // PAIR
    for j in range(chunks):
        wq_copy(j).wait()
        project(j)
        if j + SLOTS < chunks:
            wq_copy(j + SLOTS).start()
            if j == 0:
                cache_copy.start()
        elif j + SLOTS == chunks:
            for i in range(OUT_PIECES):
                wo_copy(i).start()
        for k in range(chips):
            pair_send[j, k] = part[j, row_piece(2 * k + 1 - core), :].astype(BF16)
        pair_copy(j + 1).start()
        combine(j)
        if j == PAIR + 2:
            new_token = own_sums()
            cache_copy.wait()
            attention(0)
    combine(chunks)
    acc = tokens_ref[...].astype(F32)
    for g in range(1, teams):
        attention(g)
        share(g - 1)
        acc = output(g - 1, acc)
    share(teams - 1)
    acc = output(teams - 1, acc)
    hidden_ref[...] = acc.astype(BF16)

    for s in range(chunks + 1):
        pair_copy(s).wait_send()
        for d in range(1, chips):
            far_copy(s, d).wait_send()
    for g in range(teams):
        for d in range(1, chips):
            row_copy(g, d).wait_send()
        for d in range(chips):
            twin_copy(g, d).wait_send()


def fused(lengths, tokens, norm_gain, w_query, w_keyval, w_out, cache):
    count = lax.axis_size("wide")
    chips = count // 2
    rows, width = tokens.shape
    heads = w_query.shape[1] // HEAD
    chunks = heads // GROUP
    teams = chunks // PAIR
    positions = cache.shape[1]
    vmem = pl.BlockSpec(memory_space=pltpu.VMEM)
    hbm = pl.BlockSpec(memory_space=pl.ANY)
    dma = pltpu.SemaphoreType.DMA
    kernel = functools.partial(layer_kernel, 1e-06, HEAD ** (-0.5), chips)
    hidden, fresh = pl.pallas_call(
        kernel,
        out_shape=(
            jax.ShapeDtypeStruct((rows, width), BF16),
            jax.ShapeDtypeStruct((1, 1, 4 * HALF), BF16),
        ),
        in_specs=[pl.BlockSpec(memory_space=pltpu.SMEM), vmem, vmem, hbm, hbm, hbm, hbm],
        out_specs=(vmem, vmem),
        scratch_shapes=[
            pltpu.VMEM((rows, width), BF16),
            pltpu.VMEM((SLOTS, width, GROUP * HEAD), BF16),
            pltpu.VMEM(w_keyval.shape, BF16),
            pltpu.VMEM(w_out.shape, BF16),
            pltpu.VMEM(cache.shape[1:], BF16),
            pltpu.VMEM((chunks, rows * 2 * GROUP, HALF), F32),
            pltpu.VMEM((chunks, chips, 2 * GROUP, HALF), BF16),
            pltpu.VMEM((chunks, chips, 2 * GROUP, HALF), BF16),
            pltpu.VMEM((chunks, chips, 2 * GROUP, HALF), F32),
            pltpu.VMEM((chunks, chips - 1, 2 * GROUP, HALF), BF16),
            pltpu.VMEM((chunks, chips - 1, 2 * GROUP, HALF), BF16),
            pltpu.VMEM((chips, 2, 8, HALF), F32),
            pltpu.VMEM((chips, 8, HALF), F32),
            pltpu.VMEM((chips, 8, HALF), F32),
            pltpu.VMEM((chips, 8, HALF), F32),
            pltpu.VMEM((chips - 1, 8, HALF), F32),
            pltpu.VMEM((chips - 1, 8, HALF), F32),
            pltpu.VMEM((teams, rows, TEAM, HEAD), BF16),
            pltpu.VMEM((2, rows * TEAM, HALF), F32),
            dma((SLOTS,)), dma, dma((OUT_PIECES,)), dma,
            dma((chunks + 1,)), dma((chunks + 1,)),
            dma((chunks + 1, chips - 1)), dma((chunks + 1, chips - 1)),
            dma((teams, chips - 1)), dma((teams, chips - 1)), dma((teams, chips)), dma((teams, chips)),
        ],
        compiler_params=pltpu.CompilerParams(
            collective_id=0, has_side_effects=True, vmem_limit_bytes=60 * 1024 * 1024
        ),
        cost_estimate=pl.CostEstimate(
            flops=2 * rows * width * (w_query.shape[1] * 2) + 4 * w_query.shape[1] * positions,
            bytes_accessed=2 * (w_query.size + w_out.size + cache.size),
            transcendentals=heads * positions,
        ),
    )(lengths, tokens, norm_gain.reshape(width // HALF, HALF), w_query, w_keyval, w_out, cache)
    return hidden, fresh


def masked_scores(heads_q, keys, valid, factor):
    scores = jnp.einsum("rhd,rld->rhl", heads_q, keys, preferred_element_type=F32) * factor
    return jnp.where(valid, scores, -1e30)


def attend(query, cache, fresh, lengths):
    own = query.shape[0]
    head = fresh.shape[2] // 2
    heads = query.shape[1] // head
    factor = head ** (-0.5)
    heads_q = query.reshape(own, heads, head)
    new_scores = masked_scores(heads_q, fresh[:, :, :head], True, factor)
    old_valid = (jnp.arange(cache.shape[1])[None, :] < lengths[:, None])[:, None, :]
    old_scores = masked_scores(heads_q, cache[:, :, :head], old_valid, factor)
    top = jnp.maximum(jnp.max(old_scores, axis=2), jnp.max(new_scores, axis=2))
    old_exp = jnp.where(old_valid, jnp.exp(old_scores - top[..., None]), 0.0)
    new_exp = jnp.exp(new_scores - top[..., None])
    total = jnp.sum(old_exp, axis=2) + jnp.sum(new_exp, axis=2)
    summed = jnp.einsum("rhl,rld->rhd", old_exp.astype(BF16), cache[:, :, head:], preferred_element_type=F32)
    summed = summed + jnp.einsum(
        "rhs,rsd->rhd", new_exp.astype(BF16), fresh[:, :, head:], preferred_element_type=F32
    )
    return (summed / total[..., None]).reshape(own, heads * head).astype(BF16)


def plain(lengths, tokens, norm_gain, w_query, w_keyval, w_out, cache):
    count = lax.axis_size("wide")
    own = tokens.shape[0] // count
    base_row = lax.axis_index("wide") * own
    state = tokens.astype(F32)
    scaled_in = (state * norm_gain[None, :]).astype(BF16)
    sumsq = lax.psum(jnp.sum(state * state, axis=1), "wide")
    sumsq = lax.dynamic_slice_in_dim(sumsq, base_row, own, 0)
    scale = lax.rsqrt(sumsq / (tokens.shape[1] * count) + 1e-06)[:, None]

    def project(weights):
        partial = jnp.dot(scaled_in, weights, preferred_element_type=F32)
        return (lax.psum_scatter(partial, "wide", scatter_dimension=0, tiled=True) * scale).astype(BF16)

    query = project(w_query)
    fresh = project(w_keyval)[:, None, :]
    attended = attend(query, cache, fresh, lengths)
    everything = lax.all_gather(attended, "wide", axis=0, tiled=True)
    state = state + jnp.dot(everything, w_out, preferred_element_type=F32)
    return state.astype(BF16), fresh


def on_device(tokens, norm_gain, w_query, w_keyval, w_out, cache, lengths):
    count = lax.axis_size("wide")
    fits = (
        tokens.shape[0] == count
        and count in (4, 8, 16)
        and tokens.shape[1] % HALF == 0
        and w_out.size + cache.size <= 18 * 1024 * 1024
    )
    body = fused if fits else plain
    return body(lengths, tokens, norm_gain, w_query, w_keyval, w_out, cache)


def solution(mesh):
    in_specs = (
        P("group", "wide"),
        P("wide"),
        P("wide", None),
        P("wide", None),
        P(None, "wide"),
        P(("group", "wide"), None, None),
        P(("group", "wide")),
    )
    out_specs = (P("group", "wide"), P(("group", "wide"), None, None))
    return jax.shard_map(
        on_device, mesh=mesh, in_specs=in_specs, out_specs=out_specs, check_vma=False
    )
```

```python
import functools

import jax
import jax.numpy as jnp
from jax import lax
from jax.experimental import pallas as pl
from jax.experimental.pallas import tpu as pltpu
from jax.sharding import PartitionSpec as P

MESH = pl.DeviceIdType.MESH
F32 = jnp.float32
BF16 = jnp.bfloat16
HEAD = 256
HALF = 128
GROUP = 8
PAIR = 2
TEAM = PAIR * GROUP
SLOTS = 3
OUT_PIECES = 6
COLUMNS = 4 * HEAD


def layer_kernel(
    eps, factor, chips,
    len_ref, tokens_ref, gain_ref, wq_ref, wkv_ref, wo_ref, cache_ref,
    hidden_ref, fresh_ref,
    scaled, wq_buf, wkv_buf, wo_buf, cache_buf,
    part, pair_send, pair_recv, sums, far_send, far_recv,
    kv_part, kv_pair_send, kv_pair_recv, kv_sums, kv_far_send, kv_far_recv,
    gathered, wide32, keys_t,
    wq_sem, wkv_sem, wo_sem, cache_sem,
    pair_ssem, pair_rsem, far_ssem, far_rsem,
    row_ssem, row_rsem, twin_ssem, twin_rsem,
):
    rows, width = tokens_ref.shape
    chunks = wq_ref.shape[1] // (GROUP * HEAD)
    piece = wo_ref.shape[0] // OUT_PIECES
    me = lax.axis_index("wide")
    chip, core = me // 2, me % 2
    twin = chip * 2 + 1 - core

    def peer(d):
        found, bit = 0, 1
        while bit < chips:
            own = (chip // bit) % 2
            found = found + bit * (1 - own if d & bit else own)
            bit *= 2
        return found

    def row_piece(r):
        return pl.ds(pl.multiple_of(r * 2 * GROUP, 2 * GROUP), 2 * GROUP)

    def wq_copy(j):
        return pltpu.make_async_copy(
            wq_ref.at[:, pl.ds(j * GROUP * HEAD, GROUP * HEAD)], wq_buf.at[j % SLOTS], wq_sem.at[j % SLOTS]
        )

    def wo_copy(i):
        at = pl.ds(i * piece, piece)
        return pltpu.make_async_copy(wo_ref.at[at], wo_buf.at[at], wo_sem.at[i])

    wkv_copy = pltpu.make_async_copy(wkv_ref, wkv_buf, wkv_sem)
    cache_copy = pltpu.make_async_copy(cache_ref.at[0], cache_buf, cache_sem)

    wkv_copy.start()
    for j in range(SLOTS):
        wq_copy(j).start()

    barrier = pltpu.get_barrier_semaphore()
    pl.semaphore_signal(barrier, inc=1, device_id={"wide": twin}, device_id_type=MESH)
    for d in range(1, chips):
        pl.semaphore_signal(barrier, inc=1, device_id={"wide": peer(d) * 2 + core}, device_id_type=MESH)

    state = tokens_ref[...].astype(F32)
    sumsq = jnp.sum(state * state, axis=1, keepdims=True)
    for n in range(width // HALF):
        at = slice(n * HALF, (n + 1) * HALF)
        scaled[:, at] = (state[:, at] * gain_ref[n : n + 1, :]).astype(BF16)
    pl.semaphore_wait(barrier, chips)

    def pair_copy(s):
        if s == 0:
            src, dst = kv_pair_send, kv_pair_recv
        else:
            src, dst = pair_send.at[s - 1], pair_recv.at[s - 1]
        return pltpu.make_async_remote_copy(
            src_ref=src, dst_ref=dst, send_sem=pair_ssem.at[s], recv_sem=pair_rsem.at[s],
            device_id={"wide": twin}, device_id_type=MESH,
        )

    def far_copy(s, d):
        if s == 0:
            src, dst = kv_far_send.at[d - 1], kv_far_recv.at[d - 1]
        else:
            src, dst = far_send.at[s - 1, d - 1], far_recv.at[s - 1, d - 1]
        return pltpu.make_async_remote_copy(
            src_ref=src, dst_ref=dst, send_sem=far_ssem.at[s, d - 1], recv_sem=far_rsem.at[s, d - 1],
            device_id={"wide": peer(d) * 2 + core}, device_id_type=MESH,
        )

    def combine(s):
        pair_copy(s).wait_recv()
        if s == 0:
            kv_sums[...] = kv_part[:, core] + kv_pair_recv[...]
            for d in range(1, chips):
                kv_far_send[d - 1] = kv_sums[peer(d)]
        else:
            for k in range(chips):
                sums[s - 1, k] = part[s - 1, row_piece(2 * k + core), :] + pair_recv[s - 1, k].astype(F32)
            for d in range(1, chips):
                far_send[s - 1, d - 1] = sums[s - 1, peer(d)].astype(BF16)
        for d in range(chips - 1, 0, -1):
            far_copy(s, d).start()

    wkv_copy.wait()
    keyval = jnp.dot(scaled[...], wkv_buf[...], preferred_element_type=F32)
    for r in range(rows):
        at = (r // 2, r % 2)
        for n in range(4):
            kv_part[at[0], at[1], n : n + 1, :] = keyval[r : r + 1, n * HALF : (n + 1) * HALF]
        kv_part[at[0], at[1], 4:5, :] = jnp.broadcast_to(sumsq[r : r + 1], (1, HALF))
        kv_part[at[0], at[1], 5:8, :] = jnp.zeros((3, HALF), F32)
    kv_pair_send[...] = kv_part[:, 1 - core]
    pair_copy(0).start()

    def project(j):
        slot = j % SLOTS

        def columns(n, carry):
            at = pl.ds(pl.multiple_of(n * COLUMNS, COLUMNS), COLUMNS)
            got = jnp.dot(scaled[...], wq_buf[slot, :, at], preferred_element_type=F32)
            for i in range(COLUMNS // HEAD):
                h = n * (COLUMNS // HEAD) + i
                low = got[:, i * HEAD : i * HEAD + HALF]
                high = got[:, i * HEAD + HALF : (i + 1) * HEAD]
                part[j, pl.ds(h, rows, stride=2 * GROUP), :] = low
                part[j, pl.ds(h + GROUP, rows, stride=2 * GROUP), :] = high
            return carry

        lax.fori_loop(0, GROUP * HEAD // COLUMNS, columns, 0)

    def own_sums():
        for d in range(1, chips):
            far_copy(0, d).wait_recv()
        total = kv_sums[chip]
        for d in range(1, chips):
            total = total + kv_far_recv[d - 1]
        scale = lax.rsqrt(total[4:5, :1] / (width * 2 * chips) + eps)
        keyval = (total[0:4] * scale).astype(BF16)
        for n in range(4):
            fresh_ref[0, :, n * HALF : (n + 1) * HALF] = keyval[n : n + 1]
        keyval = keyval.astype(F32)
        new_key = jnp.concatenate([keyval[0:1], keyval[1:2]], axis=1)
        new_value = jnp.concatenate([keyval[2:3], keyval[3:4]], axis=1)
        return scale, new_key, new_value

    def own_query(j):
        for d in range(1, chips):
            far_copy(j + 1, d).wait_recv()
        mine = sums[j, chip]
        for d in range(1, chips):
            mine = mine + far_recv[j, d - 1].astype(F32)
        return jnp.concatenate([mine[:GROUP], mine[GROUP:]], axis=1)

    def attention(g):
        scale, new_key, new_value = new_token
        heads_q = jnp.concatenate([own_query(g * PAIR + i) for i in range(PAIR)], axis=0)
        heads_q = (heads_q * scale).astype(BF16)
        new_score = jnp.sum(heads_q.astype(F32) * new_key, axis=1, keepdims=True) * factor
        scores = jnp.dot(heads_q, keys_t[...], preferred_element_type=F32) * factor
        valid = lax.broadcasted_iota(jnp.int32, scores.shape, 1) < len_ref[0]
        scores = jnp.where(valid, scores, -1e30)
        top = jnp.maximum(jnp.max(scores, axis=1, keepdims=True), new_score)
        exps = jnp.where(valid, jnp.exp(scores - top), 0.0)
        new_exp = jnp.exp(new_score - top)
        norm = jnp.sum(exps, axis=1, keepdims=True) + new_exp
        summed = jnp.dot(exps.astype(BF16), cache_buf[:, HEAD:], preferred_element_type=F32)
        summed = summed + new_exp.astype(BF16).astype(F32) * new_value
        gathered[g, me] = (summed / norm).astype(BF16)
        for d in range(chips - 1, 0, -1):
            row_copy(g, d).start()
        twin_copy(g, 0).start()

    def row_copy(g, d):
        return pltpu.make_async_remote_copy(
            src_ref=gathered.at[g, me], dst_ref=gathered.at[g, me],
            send_sem=row_ssem.at[g, d - 1], recv_sem=row_rsem.at[g, d - 1],
            device_id={"wide": peer(d) * 2 + core}, device_id_type=MESH,
        )

    def twin_copy(g, d):
        at = peer(d) * 2 + core
        return pltpu.make_async_remote_copy(
            src_ref=gathered.at[g, at], dst_ref=gathered.at[g, at],
            send_sem=twin_ssem.at[g, d], recv_sem=twin_rsem.at[g, d],
            device_id={"wide": twin}, device_id_type=MESH,
        )

    def share(g):
        for d in range(1, chips):
            row_copy(g, d).wait_recv()
            twin_copy(g, d).start()

    def output(g, acc):
        for d in range(chips):
            twin_copy(g, d).wait_recv()
        wide32[0] = gathered[g, :, :, :HALF].astype(F32).reshape(rows * TEAM, HALF)
        wide32[1] = gathered[g, :, :, HALF:].astype(F32).reshape(rows * TEAM, HALF)
        per = OUT_PIECES // teams
        count = COLUMNS // HEAD

        def step(n, acc):
            sides = []
            for i in range(count):
                at = pl.ds(n * count + i, rows, stride=TEAM)
                sides.append(wide32[0, at, :].astype(BF16))
                sides.append(wide32[1, at, :].astype(BF16))
            lhs = jnp.concatenate(sides, axis=1)
            at = pl.ds(pl.multiple_of(g * TEAM * HEAD + n * COLUMNS, COLUMNS), COLUMNS)
            return acc + jnp.dot(lhs, wo_buf[at, :], preferred_element_type=F32)

        steps = TEAM * HEAD // COLUMNS
        for i in range(per):
            wo_copy(g * per + i).wait()
            acc = lax.fori_loop(i * steps // per, (i + 1) * steps // per, step, acc)
        return acc

    teams = chunks // PAIR
    for j in range(chunks):
        wq_copy(j).wait()
        project(j)
        if j + SLOTS < chunks:
            wq_copy(j + SLOTS).start()
            if j == 0:
                cache_copy.start()
        elif j + SLOTS == chunks:
            for i in range(OUT_PIECES):
                wo_copy(i).start()
        for k in range(chips):
            pair_send[j, k] = part[j, row_piece(2 * k + 1 - core), :].astype(BF16)
        pair_copy(j + 1).start()
        combine(j)
        if j == PAIR + 2:
            new_token = own_sums()
            cache_copy.wait()
            keys_t[...] = cache_buf[:, :HEAD].T
            attention(0)
    combine(chunks)
    acc = tokens_ref[...].astype(F32)
    for g in range(1, teams):
        attention(g)
        share(g - 1)
    for g in range(teams - 1):
        acc = output(g, acc)
    share(teams - 1)
    acc = output(teams - 1, acc)
    hidden_ref[...] = acc.astype(BF16)

    for s in range(chunks + 1):
        pair_copy(s).wait_send()
        for d in range(1, chips):
            far_copy(s, d).wait_send()
    for g in range(teams):
        for d in range(1, chips):
            row_copy(g, d).wait_send()
        for d in range(chips):
            twin_copy(g, d).wait_send()


def fused(lengths, tokens, norm_gain, w_query, w_keyval, w_out, cache):
    count = lax.axis_size("wide")
    chips = count // 2
    rows, width = tokens.shape
    heads = w_query.shape[1] // HEAD
    chunks = heads // GROUP
    teams = chunks // PAIR
    positions = cache.shape[1]
    vmem = pl.BlockSpec(memory_space=pltpu.VMEM)
    hbm = pl.BlockSpec(memory_space=pl.ANY)
    dma = pltpu.SemaphoreType.DMA
    kernel = functools.partial(layer_kernel, 1e-06, HEAD ** (-0.5), chips)
    hidden, fresh = pl.pallas_call(
        kernel,
        out_shape=(
            jax.ShapeDtypeStruct((rows, width), BF16),
            jax.ShapeDtypeStruct((1, 1, 4 * HALF), BF16),
        ),
        in_specs=[pl.BlockSpec(memory_space=pltpu.SMEM), vmem, vmem, hbm, hbm, hbm, hbm],
        out_specs=(vmem, vmem),
        scratch_shapes=[
            pltpu.VMEM((rows, width), BF16),
            pltpu.VMEM((SLOTS, width, GROUP * HEAD), BF16),
            pltpu.VMEM(w_keyval.shape, BF16),
            pltpu.VMEM(w_out.shape, BF16),
            pltpu.VMEM(cache.shape[1:], BF16),
            pltpu.VMEM((chunks, rows * 2 * GROUP, HALF), F32),
            pltpu.VMEM((chunks, chips, 2 * GROUP, HALF), BF16),
            pltpu.VMEM((chunks, chips, 2 * GROUP, HALF), BF16),
            pltpu.VMEM((chunks, chips, 2 * GROUP, HALF), F32),
            pltpu.VMEM((chunks, chips - 1, 2 * GROUP, HALF), BF16),
            pltpu.VMEM((chunks, chips - 1, 2 * GROUP, HALF), BF16),
            pltpu.VMEM((chips, 2, 8, HALF), F32),
            pltpu.VMEM((chips, 8, HALF), F32),
            pltpu.VMEM((chips, 8, HALF), F32),
            pltpu.VMEM((chips, 8, HALF), F32),
            pltpu.VMEM((chips - 1, 8, HALF), F32),
            pltpu.VMEM((chips - 1, 8, HALF), F32),
            pltpu.VMEM((teams, rows, TEAM, HEAD), BF16),
            pltpu.VMEM((2, rows * TEAM, HALF), F32),
            pltpu.VMEM((HEAD, positions), BF16),
            dma((SLOTS,)), dma, dma((OUT_PIECES,)), dma,
            dma((chunks + 1,)), dma((chunks + 1,)),
            dma((chunks + 1, chips - 1)), dma((chunks + 1, chips - 1)),
            dma((teams, chips - 1)), dma((teams, chips - 1)), dma((teams, chips)), dma((teams, chips)),
        ],
        compiler_params=pltpu.CompilerParams(
            collective_id=0, has_side_effects=True, vmem_limit_bytes=60 * 1024 * 1024
        ),
        cost_estimate=pl.CostEstimate(
            flops=2 * rows * width * (w_query.shape[1] * 2) + 4 * w_query.shape[1] * positions,
            bytes_accessed=2 * (w_query.size + w_out.size + cache.size),
            transcendentals=heads * positions,
        ),
    )(lengths, tokens, norm_gain.reshape(width // HALF, HALF), w_query, w_keyval, w_out, cache)
    return hidden, fresh


def masked_scores(heads_q, keys, valid, factor):
    scores = jnp.einsum("rhd,rld->rhl", heads_q, keys, preferred_element_type=F32) * factor
    return jnp.where(valid, scores, -1e30)


def attend(query, cache, fresh, lengths):
    own = query.shape[0]
    head = fresh.shape[2] // 2
    heads = query.shape[1] // head
    factor = head ** (-0.5)
    heads_q = query.reshape(own, heads, head)
    new_scores = masked_scores(heads_q, fresh[:, :, :head], True, factor)
    old_valid = (jnp.arange(cache.shape[1])[None, :] < lengths[:, None])[:, None, :]
    old_scores = masked_scores(heads_q, cache[:, :, :head], old_valid, factor)
    top = jnp.maximum(jnp.max(old_scores, axis=2), jnp.max(new_scores, axis=2))
    old_exp = jnp.where(old_valid, jnp.exp(old_scores - top[..., None]), 0.0)
    new_exp = jnp.exp(new_scores - top[..., None])
    total = jnp.sum(old_exp, axis=2) + jnp.sum(new_exp, axis=2)
    summed = jnp.einsum("rhl,rld->rhd", old_exp.astype(BF16), cache[:, :, head:], preferred_element_type=F32)
    summed = summed + jnp.einsum(
        "rhs,rsd->rhd", new_exp.astype(BF16), fresh[:, :, head:], preferred_element_type=F32
    )
    return (summed / total[..., None]).reshape(own, heads * head).astype(BF16)


def plain(lengths, tokens, norm_gain, w_query, w_keyval, w_out, cache):
    count = lax.axis_size("wide")
    own = tokens.shape[0] // count
    base_row = lax.axis_index("wide") * own
    state = tokens.astype(F32)
    scaled_in = (state * norm_gain[None, :]).astype(BF16)
    sumsq = lax.psum(jnp.sum(state * state, axis=1), "wide")
    sumsq = lax.dynamic_slice_in_dim(sumsq, base_row, own, 0)
    scale = lax.rsqrt(sumsq / (tokens.shape[1] * count) + 1e-06)[:, None]

    def project(weights):
        partial = jnp.dot(scaled_in, weights, preferred_element_type=F32)
        return (lax.psum_scatter(partial, "wide", scatter_dimension=0, tiled=True) * scale).astype(BF16)

    query = project(w_query)
    fresh = project(w_keyval)[:, None, :]
    attended = attend(query, cache, fresh, lengths)
    everything = lax.all_gather(attended, "wide", axis=0, tiled=True)
    state = state + jnp.dot(everything, w_out, preferred_element_type=F32)
    return state.astype(BF16), fresh


def on_device(tokens, norm_gain, w_query, w_keyval, w_out, cache, lengths):
    count = lax.axis_size("wide")
    fits = (
        tokens.shape[0] == count
        and count in (4, 8, 16)
        and tokens.shape[1] % HALF == 0
        and w_out.size + cache.size <= 18 * 1024 * 1024
    )
    body = fused if fits else plain
    return body(lengths, tokens, norm_gain, w_query, w_keyval, w_out, cache)


def solution(mesh):
    in_specs = (
        P("group", "wide"),
        P("wide"),
        P("wide", None),
        P("wide", None),
        P(None, "wide"),
        P(("group", "wide"), None, None),
        P(("group", "wide")),
    )
    out_specs = (P("group", "wide"), P(("group", "wide"), None, None))
    return jax.shard_map(
        on_device, mesh=mesh, in_specs=in_specs, out_specs=out_specs, check_vma=False
    )
```
